512 devices in a mesh: grp: 8 (over y_lo, x), row: 64 (over z, y_hi, core).
Axes of the slice: x: 4, y: 4 (y_hi: 2, y_lo: 2; y = y_hi * 2 + y_lo), z: 16, core: 2. Of those that a mesh axis runs over, the one named last changes fastest.
Arguments:
- descriptors: bfloat16 [65536, 1024], P('row'), may hold values from -60 to 60
- sparse_points: bfloat16 [4096, 1024], P('grp'), may hold values from -60 to 60
Outputs:
- gram_slab: float32 [4096, 2048], P(('grp', 'row'))
The draws below stay inside these ranges and needn't reach their ends.
All inputs are finite; a program needn't handle non-finite values.
Results may differ from the reference program's by a relative error of at most 0.0003.
Values may be sent and summed in bfloat16 or wider, within the bound.
No kernel may reach another device: no remote copies, remote signals or barrier semaphores. Data moves between devices by JAX's collectives and lax.ppermute only.
A program may use at most 64 MiB of HBM per device.

```python
import jax
import jax.numpy as jnp
from jax import lax

D = 1024
M_BLK = 512
ROWS_DEV = 1024
ZETA = 4
M = 4096
ENVS = 65536
BAND = 4
N_GRP = 8
N_ROW = 64


def column_scales(key):
    spread = jax.random.uniform(jax.random.fold_in(key, 7), (D,), jnp.float32)
    return jnp.exp(-4.0 * spread)


def mean_spectrum(key, columns):
    level = jax.random.uniform(jax.random.fold_in(key, 9), (D,), jnp.float32, 0.5, 1.5)
    return level * columns


def cluster_centres(key, columns):
    count = max(4, M // 16)
    centre = jax.random.truncated_normal(jax.random.fold_in(key, 11), -3.0, 3.0, (count, D), jnp.float32)
    return centre * columns[None, :]


def assemble(key, count, noise, mean, centres, columns):
    label_key, scale_key = jax.random.split(key)
    labels = jax.random.randint(label_key, (count,), 0, centres.shape[0])
    row_scale = jnp.exp(jnp.log(10.0) * jax.random.uniform(scale_key, (count, 1), jnp.float32))
    values = mean[None, :] + centres[labels] + 0.7 * noise * columns[None, :]
    return (0.5 * row_scale * values).astype(jnp.bfloat16)


def draw_descriptors(key, part):
    columns = column_scales(key)
    mean = mean_spectrum(key, columns)
    centres = cluster_centres(key, columns)
    key = jax.random.fold_in(key, 1)
    noise_key = jax.random.fold_in(key, 5)
    noise = jax.random.truncated_normal(noise_key, -4.0, 4.0, (ENVS, D), jnp.float32)
    return assemble(key, ENVS, noise, mean, centres, columns)


def draw_sparse_points(key, part):
    columns = column_scales(key)
    mean = mean_spectrum(key, columns)
    centres = cluster_centres(key, columns)
    key = jax.random.fold_in(key, 2)
    noise_key = jax.random.fold_in(key, 5)
    noise = jax.random.truncated_normal(noise_key, -4.0, 4.0, (M, D), jnp.float32)
    return assemble(key, M, noise, mean, centres, columns)


def setup_inputs(seed: int = 0) -> dict:
    seeds = jax.random.split(jax.random.key(seed), 3)
    descriptors = draw_descriptors(jax.random.fold_in(seeds[2], 71), 0)
    sparse_points = draw_sparse_points(jax.random.fold_in(seeds[2], 71), 0)
    return {"descriptors": descriptors, "sparse_points": sparse_points}


kernel_variance = 24.0

def inverse_norms(values):
    floats = values.astype(jnp.float32)
    return lax.rsqrt(lax.optimization_barrier(jnp.sum(floats * floats, axis=1)) + 1e-06)

def kernel_block(left, right):
    inner = lax.dot_general(left.astype(jnp.float32), right.astype(jnp.float32), (((1,), (1,)), ((), ())), precision=lax.Precision.HIGHEST)
    cosine = inner * inverse_norms(left)[:, None] * inverse_norms(right)[None, :]
    return (kernel_variance * cosine ** ZETA).astype(jnp.bfloat16)

def reference(descriptors, sparse_points):
    blocks = descriptors.reshape(N_ROW, ROWS_DEV, D)

    def accumulate(total, rows):
        kernel = kernel_block(rows, sparse_points).astype(jnp.float32)
        grouped = kernel.reshape(ROWS_DEV, N_GRP, M_BLK)
        tiles = []
        for offset in range(BAND):
            rolled = jnp.roll(grouped, -offset, axis=1)
            tiles.append(jnp.einsum('rai,rac->aic', grouped, rolled, precision=lax.Precision.HIGHEST))
        slab = jnp.stack(tiles, axis=2).reshape(N_GRP * M_BLK, BAND * M_BLK)
        return (total + slab, None)
    start = jnp.zeros((N_GRP * M_BLK, BAND * M_BLK), jnp.float32)
    total, _ = lax.scan(accumulate, start, blocks)
    return total / ENVS
```

```python
import functools

import jax
import jax.numpy as jnp
from jax import lax
from jax.experimental import pallas as pl
from jax.experimental.pallas import tpu as pltpu
from jax.sharding import Mesh
from jax.sharding import PartitionSpec as P

NAMES = ("y_lo", "x", "z_hi", "z_lo", "y_hi", "core")
SIZES = (2, 4, 8, 2, 2, 2)
KERNEL_VARIANCE = 24.0
D = 1024
ENV = 1024
BLK = 512
HALF = BLK // 2
WIDE = 4 * HALF
TARGET = 14
VMEM = 60 * 1024 * 1024


def flat(y_lo, x, z_hi, z_lo, y_hi, core):
    return ((((y_lo * 4 + x) * 8 + z_hi) * 2 + z_lo) * 2 + y_hi) * 2 + core


def from_group(steps):
    pairs = []
    for y_lo in range(2):
        for x in range(4):
            source = (y_lo * 4 + x + steps) % 8
            s_lo, s_x = divmod(source, 4)
            for z_hi in range(8):
                for z_lo in range(2):
                    for y_hi in range(2):
                        for core in range(2):
                            y = y_hi * 2 + y_lo
                            if s_lo != y_lo:
                                y = (y + (1 if core == 0 else -1)) % 4
                            pairs.append((flat(s_lo, s_x, z_hi, z_lo, y // 2, core), flat(y_lo, x, z_hi, z_lo, y_hi, core)))
    return pairs


def whole(*shape):
    return pl.BlockSpec(memory_space=pltpu.VMEM)


def call(body, outs, inputs, scratch=(), flops=0):
    size = sum(v.size * v.dtype.itemsize for v in inputs)
    return pl.pallas_call(
        body,
        out_shape=outs,
        in_specs=[pl.BlockSpec(memory_space=pltpu.VMEM)] * len(inputs),
        out_specs=jax.tree.map(lambda _: pl.BlockSpec(memory_space=pltpu.VMEM), outs),
        scratch_shapes=list(scratch),
        compiler_params=pltpu.CompilerParams(vmem_limit_bytes=VMEM),
        cost_estimate=pl.CostEstimate(flops=flops, bytes_accessed=size, transcendentals=0),
    )(*inputs)


def nt(left, right):
    return lax.dot_general(left, right, (((1,), (1,)), ((), ())), preferred_element_type=jnp.float32)


def point_inverse(points):
    floats = points.astype(jnp.float32)
    return lax.rsqrt(jnp.sum(floats * floats, axis=1, keepdims=True) + 1e-06)


def powered(inner, left_inv, right_inv):
    cosine = inner * left_inv * right_inv
    square = cosine * cosine
    return (KERNEL_VARIANCE * (square * square)).astype(jnp.bfloat16)


def own_kernel(points, rows, rows_inv, out):
    inv = point_inverse(points[...])

    @pl.loop(0, ENV // 256)
    def _(i):
        part = pl.ds(pl.multiple_of(i * 256, 256), 256)
        out[:, part] = powered(nt(points[...], rows[part, :]), inv, rows_inv[:, part])


def exponent(largest):
    return jnp.floor(jnp.log2(jnp.maximum(largest, 1e-37)))


def coded(values, e, rows, width):
    half = jnp.exp2(0.5 * (TARGET - e))
    scaled = values * half * half
    scaled = scaled * scaled
    scaled = scaled * scaled
    scaled = scaled * scaled
    row = lax.broadcasted_iota(jnp.int32, values.shape, 0)
    lane = lax.broadcasted_iota(jnp.int32, values.shape, 1)
    number = jnp.broadcast_to(e.astype(jnp.int32) + 128, values.shape)
    bit = lax.shift_right_logical(number, jnp.minimum(lane, 30)) & 1
    marked = (row % rows == 0) & (lane < 8)
    scaled = jnp.where(marked, jnp.maximum(scaled, 1e-35), scaled)
    return jnp.where(marked & (bit == 1), -scaled, scaled).astype(jnp.bfloat16)


def decoded(chunk):
    floats = chunk.astype(jnp.float32)
    head = floats[0:1, 0:128]
    lane = lax.broadcasted_iota(jnp.int32, head.shape, 1)
    weight = jnp.left_shift(1, jnp.minimum(lane, 7)).astype(jnp.float32)
    number = jnp.sum(jnp.where((lane < 8) & (head < 0), weight, 0.0), axis=1, keepdims=True)
    return jnp.exp2(jnp.log2(jnp.abs(floats)) * 0.125 + (number - (128 + TARGET)))


def gram_kernel(core, a0, a1, d0, d1, e0, e1, b1, b2_low, b2_high, b3, out, points, k0, k1, gram):
    points[0:256, :] = b1[...]
    points[256:384, :] = b2_low[...]
    points[384:512, :] = b2_high[...]
    points[512:768, :] = b3[...]
    inv = point_inverse(points[...])
    mine = pl.ds(pl.multiple_of(core[0] * HALF, HALF), HALF)
    for a, rows, rows_inv, k in ((a0, d0, e0, k0), (a1, d1, e1, k1)):
        k[0:HALF, :] = a[mine, :]

        @pl.loop(0, ENV // 256)
        def _(i):
            part = pl.ds(pl.multiple_of(i * 256, 256), 256)
            k[HALF:, part] = powered(nt(points[...], rows[part, :]), inv, rows_inv[:, part])

    def step(i, largest):
        part = pl.ds(pl.multiple_of(i * 128, 128), 128)
        block = nt(a0[part, :], k0[...]) + nt(a1[part, :], k1[...])
        gram[part, :] = block
        return jnp.maximum(largest, jnp.max(block, axis=(0, 1), keepdims=True))

    e = exponent(lax.fori_loop(0, BLK // 128, step, jnp.zeros((1, 1), jnp.float32)))

    @pl.loop(0, 8)
    def _(z_hi):
        for d in range(4):
            values = gram[pl.ds(pl.multiple_of(z_hi * 64 + d * 16, 16), 16), :]
            out[pl.ds(pl.multiple_of(d * 128 + z_hi * 16, 16), 16), :] = coded(values, e, 16, WIDE)


def middle_kernel(chunks, out):
    total = decoded(chunks[0:128, :])
    for s in range(1, 4):
        total = total + decoded(chunks[s * 128 : (s + 1) * 128, :])
    e = exponent(jnp.max(total, axis=(0, 1), keepdims=True))
    out[...] = coded(total, e, 8, WIDE)


def last_kernel(scale, chunks, out):
    for core in range(2):
        total = jnp.zeros((8, WIDE), jnp.float32)
        for z_hi in range(8):
            total = total + decoded(chunks[z_hi * 2 + core, :, :])
        total = total * scale
        for j in range(4):
            out[:, j * BLK + core * HALF : j * BLK + (core + 1) * HALF] = total[:, j * HALF : (j + 1) * HALF]


def env_inverse(rows):
    floats = rows.astype(jnp.float32)
    return lax.rsqrt(jnp.sum(floats * floats, axis=1) + 1e-06).reshape(1, ENV)


def shards(descriptors, sparse_points):
    f32, bf16 = jnp.float32, jnp.bfloat16
    core = lax.axis_index("core")
    mine = lax.dynamic_slice_in_dim(sparse_points, core * HALF, HALF, 0)
    b1 = lax.ppermute(mine, NAMES, from_group(1))
    b3 = lax.ppermute(mine, NAMES, from_group(3))
    other = lax.ppermute(descriptors, "core", [(0, 1), (1, 0)])
    b2_low = lax.ppermute(b1[: HALF // 2], NAMES, from_group(1))
    b2_high = lax.ppermute(b3[HALF // 2 :], NAMES, from_group(-1))

    columns = []
    for rows in (descriptors, other):
        inv = env_inverse(rows)
        own = call(
            own_kernel, jax.ShapeDtypeStruct((BLK, ENV), bf16), (sparse_points, rows, inv), flops=2 * BLK * ENV * D
        )
        columns.append((own, rows, inv))
    (a0, d0, e0), (a1, d1, e1) = columns

    number = core.astype(jnp.int32).reshape(1)
    inputs = (number, a0, a1, d0, d1, e0, e1, b1, b2_low, b2_high, b3)
    sent = pl.pallas_call(
        gram_kernel,
        out_shape=jax.ShapeDtypeStruct((BLK, WIDE), bf16),
        in_specs=[pl.BlockSpec(memory_space=pltpu.SMEM)] + [pl.BlockSpec(memory_space=pltpu.VMEM)] * 10,
        out_specs=pl.BlockSpec(memory_space=pltpu.VMEM),
        scratch_shapes=[
            pltpu.VMEM((3 * HALF, D), bf16),
            pltpu.VMEM((WIDE, ENV), bf16),
            pltpu.VMEM((WIDE, ENV), bf16),
            pltpu.VMEM((BLK, WIDE), f32),
        ],
        compiler_params=pltpu.CompilerParams(vmem_limit_bytes=VMEM),
        cost_estimate=pl.CostEstimate(flops=10 * 2**30, bytes_accessed=12 * 2**20, transcendentals=0),
    )(*inputs)
    got = lax.all_to_all(sent, ("z_lo", "y_hi"), 0, 0, tiled=True)
    sent = call(middle_kernel, jax.ShapeDtypeStruct((128, WIDE), bf16), (got,))
    got = lax.all_to_all(sent.reshape(16, 8, WIDE), ("z_hi", "core"), 0, 0, tiled=True)
    scale = 1.0 / (ENV * 64)
    return call(functools.partial(last_kernel, scale), jax.ShapeDtypeStruct((8, 4 * BLK), f32), (got,))


def solution(mesh):
    fine = Mesh(mesh.devices.reshape(SIZES), NAMES)
    return jax.shard_map(
        shards,
        mesh=fine,
        in_specs=(P(("z_hi", "z_lo", "y_hi", "core"), None), P(("y_lo", "x"), None)),
        out_specs=P(NAMES, None),
        check_vma=False,
    )
```

```python
import functools

import jax
import jax.numpy as jnp
from jax import lax
from jax.experimental import pallas as pl
from jax.experimental.pallas import tpu as pltpu
from jax.sharding import Mesh
from jax.sharding import PartitionSpec as P

NAMES = ("y_lo", "x", "z_hi", "z_lo", "y_hi", "core")
SIZES = (2, 4, 8, 2, 2, 2)
KERNEL_VARIANCE = 24.0
D = 1024
ENV = 1024
BLK = 512
HALF = BLK // 2
WIDE = 4 * HALF
TARGET = 14
VMEM = 24 * 1024 * 1024


def flat(y_lo, x, z_hi, z_lo, y_hi, core):
    return ((((y_lo * 4 + x) * 8 + z_hi) * 2 + z_lo) * 2 + y_hi) * 2 + core


def from_group(steps, same_row=False):
    pairs = []
    for y_lo in range(2):
        for x in range(4):
            source = (y_lo * 4 + x + steps) % 8
            s_lo, s_x = divmod(source, 4)
            for z_hi in range(8):
                for z_lo in range(2):
                    for y_hi in range(2):
                        for core in range(2):
                            y = y_hi * 2 + y_lo
                            if s_lo != y_lo and not same_row:
                                y = (y + (1 if core == 0 else -1)) % 4
                            s_hi = y_hi if same_row else y // 2
                            pairs.append((flat(s_lo, s_x, z_hi, z_lo, s_hi, core), flat(y_lo, x, z_hi, z_lo, y_hi, core)))
    return pairs


def call(body, outs, inputs, scratch=(), flops=0):
    size = sum(v.size * v.dtype.itemsize for v in inputs)
    whole = pl.BlockSpec(memory_space=pltpu.VMEM)
    return pl.pallas_call(
        body,
        out_shape=outs,
        in_specs=[pl.BlockSpec(memory_space=pltpu.SMEM) if v.dtype == jnp.int32 else whole for v in inputs],
        out_specs=jax.tree.map(lambda _: whole, outs),
        scratch_shapes=list(scratch),
        compiler_params=pltpu.CompilerParams(vmem_limit_bytes=VMEM),
        cost_estimate=pl.CostEstimate(flops=flops, bytes_accessed=size, transcendentals=0),
    )(*inputs)


def nt(left, right):
    return lax.dot_general(left, right, (((1,), (1,)), ((), ())), preferred_element_type=jnp.float32)


def inverse(values):
    floats = values.astype(jnp.float32)
    return lax.rsqrt(jnp.sum(floats * floats, axis=1, keepdims=True) + 1e-06)


def powered(inner, left_inv, right_inv):
    cosine = inner * left_inv * right_inv
    square = cosine * cosine
    return (KERNEL_VARIANCE * (square * square)).astype(jnp.bfloat16)


def own_kernel(points, rows, out, rows_inv):
    inv = inverse(points[...])
    for i in range(ENV // 256):
        part = slice(i * 256, (i + 1) * 256)
        column = inverse(rows[part, :])
        line = jnp.broadcast_to(column, (256, 128)).T[0:1, :]
        rows_inv[:, part] = line
        out[:, part] = powered(nt(points[...], rows[part, :]), inv, line)


def next_kernel(b, c, d0, d1, e0, e1, k0, k1):
    b_inv, c_inv = inverse(b[...]), inverse(c[...])
    for rows, rows_inv, k in ((d0, e0, k0), (d1, e1, k1)):
        for i in range(ENV // 256):
            part = slice(i * 256, (i + 1) * 256)
            k[0:HALF, part] = powered(nt(b[...], rows[part, :]), b_inv, rows_inv[:, part])
            k[HALF:BLK, part] = powered(nt(c[...], rows[part, :]), c_inv, rows_inv[:, part])


def exponent(largest):
    return jnp.floor(jnp.log2(jnp.maximum(largest, 1e-37)))


def coded(values, half):
    scaled = values * half * half
    scaled = scaled * scaled
    scaled = scaled * scaled
    return scaled * scaled


def marked(scaled, e, rows):
    row = lax.broadcasted_iota(jnp.int32, scaled.shape, 0)
    lane = lax.broadcasted_iota(jnp.int32, scaled.shape, 1)
    number = jnp.broadcast_to(e.astype(jnp.int32) + 128, scaled.shape)
    bit = lax.shift_right_logical(number, jnp.minimum(lane, 30)) & 1
    head = (row % rows == 0) & (lane < 8)
    scaled = jnp.where(head, jnp.maximum(scaled, 1e-35), scaled)
    return jnp.where(head & (bit == 1), -scaled, scaled)


def shift(head):
    floats = head.astype(jnp.float32)
    lane = lax.broadcasted_iota(jnp.int32, floats.shape, 1)
    weight = jnp.left_shift(1, jnp.minimum(lane, 7)).astype(jnp.float32)
    number = jnp.sum(jnp.where((lane < 8) & (floats < 0), weight, 0.0), axis=1, keepdims=True)
    return number - (128 + TARGET)


def decoded(values, add):
    return jnp.exp2(jnp.log2(jnp.abs(values.astype(jnp.float32))) * 0.125 + add)


def gram_kernel(core, a0, a1, n0, n1, d0, d1, e0, e1, b, out, k0, k1, gram):
    mine = pl.ds(pl.multiple_of(core[0] * HALF, HALF), HALF)
    rest = pl.ds(pl.multiple_of((1 - core[0]) * HALF, HALF), HALF)
    inv = inverse(b[...])
    for rows, rows_inv, n, k in ((d0, e0, n0, k0), (d1, e1, n1, k1)):
        k[mine, :] = n[0:HALF, :]
        for i in range(ENV // 256):
            part = slice(i * 256, (i + 1) * 256)
            k[rest, part] = powered(nt(b[...], rows[part, :]), inv, rows_inv[:, part])
    largest = jnp.zeros((1, HALF), jnp.float32)
    for j, (l0, l1, r0, r1, part) in enumerate(
        (
            (a0, a1, a0, a1, mine),
            (a0, a1, n0, n1, slice(0, HALF)),
            (k0, k1, n0, n1, slice(HALF, BLK)),
            (a0, a1, n0, n1, slice(HALF, BLK)),
        )
    ):
        block = nt(l0[...], r0[part, :]) + nt(l1[...], r1[part, :])
        gram[:, j * HALF : (j + 1) * HALF] = block
        largest = jnp.maximum(largest, jnp.max(block, axis=0, keepdims=True))
    e = exponent(jnp.max(largest, axis=1, keepdims=True))
    half = jnp.exp2(0.5 * (TARGET - e))
    for z_hi in range(8):
        for d in range(4):
            values = coded(gram[z_hi * 64 + d * 16 : z_hi * 64 + (d + 1) * 16, :], half)
            to = slice(d * 128 + z_hi * 16, d * 128 + (z_hi + 1) * 16)
            out[to, :] = values.astype(jnp.bfloat16)
            if z_hi == 0:
                out[to, 0:128] = marked(values[:, 0:128], e, 16).astype(jnp.bfloat16)


def middle_kernel(chunks, out):
    total = jnp.zeros((128, WIDE), jnp.float32)
    for s in range(4):
        total = total + decoded(chunks[s * 128 : (s + 1) * 128, :], shift(chunks[s * 128 : s * 128 + 16, 0:128])[0:1])
    e = exponent(jnp.max(jnp.max(total, axis=0, keepdims=True), axis=1, keepdims=True))
    values = coded(total, jnp.exp2(0.5 * (TARGET - e)))
    out[...] = values.astype(jnp.bfloat16)
    out[:, 0:128] = marked(values[:, 0:128], e, 8).astype(jnp.bfloat16)


def last_kernel(tiles, scale, chunks, out):
    for core in range(2):
        adds = [shift(chunks[z_hi * 2 + core, :, 0:128])[0:1] for z_hi in range(8)]
        for tile, to in tiles:
            part = slice(tile * HALF, (tile + 1) * HALF)
            total = jnp.zeros((8, HALF), jnp.float32)
            for z_hi in range(8):
                total = total + decoded(chunks[z_hi * 2 + core, :, part], adds[z_hi])
            out[:, to * BLK + core * HALF : to * BLK + (core + 1) * HALF] = total * scale


def shards(descriptors, sparse_points):
    f32, bf16 = jnp.float32, jnp.bfloat16
    core = lax.axis_index("core")
    swap = [(0, 1), (1, 0)]
    mine = lax.dynamic_slice_in_dim(sparse_points, core * HALF, HALF, 0)
    b = lax.ppermute(mine, NAMES, from_group(1))
    c = lax.ppermute(mine, NAMES, from_group(3))
    other = lax.ppermute(descriptors, "core", swap)

    one = jax.ShapeDtypeStruct((BLK, ENV), bf16)
    line = jax.ShapeDtypeStruct((1, ENV), f32)
    a0, e0 = call(own_kernel, (one, line), (sparse_points, descriptors), flops=2 * BLK * ENV * D)
    a1, e1 = call(own_kernel, (one, line), (sparse_points, other), flops=2 * BLK * ENV * D)
    b, a0, a1 = lax.optimization_barrier((b, a0, a1))
    b_rest = lax.ppermute(b, "core", swap)
    n0, n1 = call(next_kernel, (one, one), (b, c, descriptors, other, e0, e1), flops=4 * BLK * ENV * D)
    sent = call(
        gram_kernel,
        jax.ShapeDtypeStruct((BLK, WIDE), bf16),
        (core.astype(jnp.int32).reshape(1), a0, a1, n0, n1, descriptors, other, e0, e1, b_rest),
        [pltpu.VMEM((BLK, ENV), bf16), pltpu.VMEM((BLK, ENV), bf16), pltpu.VMEM((BLK, WIDE), f32)],
        flops=6 * BLK * ENV * D,
    )
    got = lax.all_to_all(sent, ("z_lo", "y_hi"), 0, 0, tiled=True)
    sent = call(middle_kernel, jax.ShapeDtypeStruct((128, WIDE), bf16), (got,))
    got = lax.all_to_all(sent.reshape(16, 8, WIDE), ("z_hi", "core"), 0, 0, tiled=True)
    scale = 1.0 / (ENV * 64)
    later = call(functools.partial(last_kernel, ((2, 0),), scale), jax.ShapeDtypeStruct((8, BLK), f32), (got,))
    later = lax.ppermute(later, NAMES, from_group(-1, same_row=True))
    tiles = ((0, 0), (1, 1), (3, 3))
    out = call(functools.partial(last_kernel, tiles, scale), jax.ShapeDtypeStruct((8, 4 * BLK), f32), (got,))
    return lax.dynamic_update_slice(out, later, (0, 2 * BLK))


def solution(mesh):
    fine = Mesh(mesh.devices.reshape(SIZES), NAMES)
    return jax.shard_map(
        shards,
        mesh=fine,
        in_specs=(P(("z_hi", "z_lo", "y_hi", "core"), None), P(("y_lo", "x"), None)),
        out_specs=P(NAMES, None),
        check_vma=False,
    )
```

```python
import functools

import jax
import jax.numpy as jnp
from jax import lax
from jax.experimental import pallas as pl
from jax.experimental.pallas import tpu as pltpu
from jax.sharding import Mesh
from jax.sharding import PartitionSpec as P

NAMES = ("y_lo", "x", "z_hi", "z_lo", "y_hi", "core")
SIZES = (2, 4, 8, 2, 2, 2)
KERNEL_VARIANCE = 24.0
D = 1024
ENV = 1024
BLK = 512
HALF = BLK // 2
WIDE = 4 * HALF
TARGET = 14
VMEM = 24 * 1024 * 1024


def flat(y_lo, x, z_hi, z_lo, y_hi, core):
    return ((((y_lo * 4 + x) * 8 + z_hi) * 2 + z_lo) * 2 + y_hi) * 2 + core


def from_group(steps, same_row=False):
    pairs = []
    for y_lo in range(2):
        for x in range(4):
            source = (y_lo * 4 + x + steps) % 8
            s_lo, s_x = divmod(source, 4)
            for z_hi in range(8):
                for z_lo in range(2):
                    for y_hi in range(2):
                        for core in range(2):
                            y = y_hi * 2 + y_lo
                            if s_lo != y_lo and not same_row:
                                y = (y + (1 if core == 0 else -1)) % 4
                            s_hi = y_hi if same_row else y // 2
                            pairs.append((flat(s_lo, s_x, z_hi, z_lo, s_hi, core), flat(y_lo, x, z_hi, z_lo, y_hi, core)))
    return pairs


def call(body, outs, inputs, scratch=(), flops=0):
    size = sum(v.size * v.dtype.itemsize for v in inputs)
    whole = pl.BlockSpec(memory_space=pltpu.VMEM)
    return pl.pallas_call(
        body,
        out_shape=outs,
        in_specs=[pl.BlockSpec(memory_space=pltpu.SMEM) if v.dtype == jnp.int32 else whole for v in inputs],
        out_specs=jax.tree.map(lambda _: whole, outs),
        scratch_shapes=list(scratch),
        compiler_params=pltpu.CompilerParams(vmem_limit_bytes=VMEM),
        cost_estimate=pl.CostEstimate(flops=flops, bytes_accessed=size, transcendentals=0),
    )(*inputs)


def nt(left, right):
    return lax.dot_general(left, right, (((1,), (1,)), ((), ())), preferred_element_type=jnp.float32)


def inverse(values):
    floats = values.astype(jnp.float32)
    return lax.rsqrt(jnp.sum(floats * floats, axis=1, keepdims=True) + 1e-06)


def powered(inner, left_inv, right_inv):
    cosine = inner * left_inv * right_inv
    square = cosine * cosine
    return (KERNEL_VARIANCE * (square * square)).astype(jnp.bfloat16)


def half_kernel(core, points, out, sem):
    mine = pl.ds(pl.multiple_of(core[0] * HALF, HALF), HALF)
    copy = pltpu.make_async_copy(points.at[mine, :], out, sem)
    copy.start()
    copy.wait()


def own_columns(points, inv, rows, part, out, rows_inv):
    line = jnp.broadcast_to(inverse(rows[part, :]), (256, 128)).T[0:1, :]
    rows_inv[:, part] = line
    out[:, part] = powered(nt(points[...], rows[part, :]), inv, line)


def first_kernel(points_far, rows_far, out, rows_inv, points, rows, sems):
    parts = [slice(i * 256, (i + 1) * 256) for i in range(ENV // 256)]
    copies = [pltpu.make_async_copy(points_far, points, sems.at[4])]
    copies += [pltpu.make_async_copy(rows_far.at[p, :], rows.at[p, :], sems.at[i]) for i, p in enumerate(parts)]
    for copy in copies:
        copy.start()
    copies[0].wait()
    inv = inverse(points[...])
    for copy, part in zip(copies[1:], parts):
        copy.wait()
        own_columns(points, inv, rows, part, out, rows_inv)


def tile(left, right):
    return nt(left[0], right[0]) + nt(left[1], right[1])


def fill(points, inv, rows, rows_inv, out):
    for i in range(ENV // 256):
        part = slice(i * 256, (i + 1) * 256)
        out[:, part] = powered(nt(points[...], rows[part, :]), inv, rows_inv[:, part])


def second_kernel(core, points, rows, a0, a1, rows_inv, gram):
    inv = inverse(points[...])
    for i in range(ENV // 256):
        own_columns(points, inv, rows, slice(i * 256, (i + 1) * 256), a1, rows_inv)
    mine = pl.ds(pl.multiple_of(core[0] * HALF, HALF), HALF)
    gram[...] = tile((a0[...], a1[...]), (a0[mine, :], a1[mine, :]))


def next_kernel(b, d0, d1, e0, e1, a0, a1, b0, b1, gram):
    inv = inverse(b[...])
    fill(b, inv, d0, e0, b0)
    fill(b, inv, d1, e1, b1)
    gram[...] = tile((a0[...], a1[...]), (b0[...], b1[...]))


def exponent(largest):
    return jnp.floor(jnp.log2(jnp.maximum(largest, 1e-37)))


def coded(values, half):
    scaled = values * half * half
    scaled = scaled * scaled
    scaled = scaled * scaled
    return scaled * scaled


def marked(scaled, e, rows):
    row = lax.broadcasted_iota(jnp.int32, scaled.shape, 0)
    lane = lax.broadcasted_iota(jnp.int32, scaled.shape, 1)
    number = jnp.broadcast_to(e.astype(jnp.int32) + 128, scaled.shape)
    bit = lax.shift_right_logical(number, jnp.minimum(lane, 30)) & 1
    head = (row % rows == 0) & (lane < 8)
    scaled = jnp.where(head, jnp.maximum(scaled, 1e-35), scaled)
    return jnp.where(head & (bit == 1), -scaled, scaled)


def shift(head):
    floats = head.astype(jnp.float32)
    lane = lax.broadcasted_iota(jnp.int32, floats.shape, 1)
    weight = jnp.left_shift(1, jnp.minimum(lane, 7)).astype(jnp.float32)
    number = jnp.sum(jnp.where((lane < 8) & (floats < 0), weight, 0.0), axis=1, keepdims=True)
    return number - (128 + TARGET)


def decoded(values, add):
    return jnp.exp2(jnp.log2(jnp.abs(values.astype(jnp.float32))) * 0.125 + add)


def gram_kernel(core, g_aa, g_ab, a0, a1, b0, b1, c, rest, d0, d1, e0, e1, out, c0, c1, k0, k1, gram):
    mine = pl.ds(pl.multiple_of(core[0] * HALF, HALF), HALF)
    others = pl.ds(pl.multiple_of((1 - core[0]) * HALF, HALF), HALF)
    c_inv, rest_inv = inverse(c[...]), inverse(rest[...])
    for rows, rows_inv, out_c, old, k in ((d0, e0, c0, b0, k0), (d1, e1, c1, b1, k1)):
        fill(c, c_inv, rows, rows_inv, out_c)
        k[mine, :] = old[...]
        for i in range(ENV // 256):
            part = slice(i * 256, (i + 1) * 256)
            k[others, part] = powered(nt(rest[...], rows[part, :]), rest_inv, rows_inv[:, part])
    columns = (c0[...], c1[...])
    ac = tile((a0[...], a1[...]), columns)
    bc = tile((k0[...], k1[...]), columns)
    gram[:, 0:HALF] = ac
    gram[:, HALF:BLK] = bc
    largest = jnp.maximum(
        jnp.maximum(jnp.max(ac, axis=0, keepdims=True), jnp.max(bc, axis=0, keepdims=True)),
        jnp.maximum(jnp.max(g_aa[...], axis=0, keepdims=True), jnp.max(g_ab[...], axis=0, keepdims=True)),
    )
    e = exponent(jnp.max(largest, axis=1, keepdims=True))
    half = jnp.exp2(0.5 * (TARGET - e))
    for d in range(8):
        for pair in range(4):
            starts = [(2 * pair + i) * 64 + d * 8 for i in range(2)]
            to = slice(d * 64 + pair * 16, d * 64 + (pair + 1) * 16)
            column = 0
            for source in (g_aa, g_ab, gram):
                width = source.shape[1]
                values = coded(jnp.concatenate([source[r : r + 8, :] for r in starts], axis=0), half)
                out[to, column : column + width] = values.astype(jnp.bfloat16)
                if pair == 0 and column == 0:
                    out[to, 0:128] = marked(values[:, 0:128], e, 16).astype(jnp.bfloat16)
                column += width


def middle_kernel(chunks, out):
    totals = []
    for core in range(2):
        total = jnp.zeros((64, WIDE), jnp.float32)
        for s in range(core, 8, 2):
            add = shift(chunks[s * 64 : s * 64 + 16, 0:128])[0:1]
            total = total + decoded(chunks[s * 64 : (s + 1) * 64, :], add)
        totals.append(total)
    largest = jnp.maximum(jnp.max(totals[0], axis=0, keepdims=True), jnp.max(totals[1], axis=0, keepdims=True))
    e = exponent(jnp.max(largest, axis=1, keepdims=True))
    half = jnp.exp2(0.5 * (TARGET - e))
    for core in range(2):
        values = coded(totals[core], half)
        out[:, core * WIDE : (core + 1) * WIDE] = values.astype(jnp.bfloat16)
        if core == 0:
            out[:, 0:128] = marked(values[:, 0:128], e, 8).astype(jnp.bfloat16)


def last_kernel(tiles, scale, chunks, out):
    adds = [shift(chunks[z_hi, :, 0:128])[0:1] for z_hi in range(8)]
    for core in range(2):
        for source, to in tiles:
            part = slice(core * WIDE + source * HALF, core * WIDE + (source + 1) * HALF)
            total = jnp.zeros((8, HALF), jnp.float32)
            for z_hi in range(8):
                total = total + decoded(chunks[z_hi, :, part], adds[z_hi])
            out[:, to * BLK + core * HALF : to * BLK + (core + 1) * HALF] = total * scale


def shards(descriptors, sparse_points):
    f32, bf16 = jnp.float32, jnp.bfloat16
    core = lax.axis_index("core")
    number = core.astype(jnp.int32).reshape(1)
    swap = [(0, 1), (1, 0)]
    one = jax.ShapeDtypeStruct((BLK, ENV), bf16)
    half = jax.ShapeDtypeStruct((HALF, ENV), bf16)
    line = jax.ShapeDtypeStruct((1, ENV), f32)
    gram = jax.ShapeDtypeStruct((BLK, HALF), f32)
    work = 2 * BLK * ENV * D
    far = pl.BlockSpec(memory_space=pltpu.HBM)
    points_far = pltpu.with_memory_space_constraint(sparse_points, pltpu.HBM)
    rows_far = pltpu.with_memory_space_constraint(descriptors, pltpu.HBM)
    whole = pl.BlockSpec(memory_space=pltpu.VMEM)
    mine = pl.pallas_call(
        half_kernel,
        out_shape=jax.ShapeDtypeStruct((HALF, D), bf16),
        in_specs=[pl.BlockSpec(memory_space=pltpu.SMEM), far],
        out_specs=whole,
        scratch_shapes=[pltpu.SemaphoreType.DMA],
        compiler_params=pltpu.CompilerParams(vmem_limit_bytes=VMEM),
    )(number, points_far)
    b = lax.ppermute(mine, NAMES, from_group(1))
    c = lax.ppermute(mine, NAMES, from_group(3))
    a0, e0 = pl.pallas_call(
        first_kernel,
        out_shape=(one, line),
        in_specs=[far, far],
        out_specs=(whole, whole),
        scratch_shapes=[pltpu.VMEM((BLK, D), bf16), pltpu.VMEM((ENV, D), bf16), pltpu.SemaphoreType.DMA((5,))],
        compiler_params=pltpu.CompilerParams(vmem_limit_bytes=VMEM),
        cost_estimate=pl.CostEstimate(flops=work, bytes_accessed=3 * 2**20, transcendentals=0),
    )(points_far, rows_far)
    other = lax.ppermute(descriptors, "core", swap)
    a1, e1, g_aa = call(second_kernel, (one, line, gram), (number, sparse_points, other, a0), flops=work * 3 // 2)
    b, a1, g_aa = lax.optimization_barrier((b, a1, g_aa))
    rest = lax.ppermute(b, "core", swap)
    b0, b1, g_ab = call(next_kernel, (half, half, gram), (b, descriptors, other, e0, e1, a0, a1), flops=work * 3 // 2)
    sent = call(
        gram_kernel,
        jax.ShapeDtypeStruct((BLK, WIDE), bf16),
        (number, g_aa, g_ab, a0, a1, b0, b1, c, rest, descriptors, other, e0, e1),
        [pltpu.VMEM((HALF, ENV), bf16)] * 2 + [pltpu.VMEM((BLK, ENV), bf16)] * 2 + [pltpu.VMEM((BLK, BLK), f32)],
        flops=work * 3,
    )
    got = lax.all_to_all(sent, ("z_lo", "y_hi", "core"), 0, 0, tiled=True)
    sent = call(middle_kernel, jax.ShapeDtypeStruct((64, 2 * WIDE), bf16), (got,))
    got = lax.all_to_all(sent.reshape(8, 8, 2 * WIDE), "z_hi", 0, 0, tiled=True)
    scale = 1.0 / (ENV * 64)
    ahead = call(functools.partial(last_kernel, ((3, 0),), scale), jax.ShapeDtypeStruct((8, BLK), f32), (got,))
    ahead = lax.ppermute(ahead, NAMES, from_group(-1, same_row=True))
    tiles = ((0, 0), (1, 1), (2, 3))
    out = call(functools.partial(last_kernel, tiles, scale), jax.ShapeDtypeStruct((8, 4 * BLK), f32), (got,))
    return lax.dynamic_update_slice(out, ahead, (0, 2 * BLK))


def solution(mesh):
    fine = Mesh(mesh.devices.reshape(SIZES), NAMES)
    return jax.shard_map(
        shards,
        mesh=fine,
        in_specs=(P(("z_hi", "z_lo", "y_hi", "core"), None), P(("y_lo", "x"), None)),
        out_specs=P(NAMES, None),
        check_vma=False,
    )
```

```python
import functools

import jax
import jax.numpy as jnp
from jax import lax
from jax.experimental import pallas as pl
from jax.experimental.pallas import tpu as pltpu
from jax.sharding import Mesh
from jax.sharding import PartitionSpec as P

NAMES = ("y_lo", "x", "z_hi", "z_lo", "y_hi", "core")
SIZES = (2, 4, 8, 2, 2, 2)
KERNEL_VARIANCE = 24.0
D = 1024
ENV = 1024
BLK = 512
HALF = BLK // 2
WIDE = 4 * HALF
TARGET = 14
VMEM = 24 * 1024 * 1024


def flat(y_lo, x, z_hi, z_lo, y_hi, core):
    return ((((y_lo * 4 + x) * 8 + z_hi) * 2 + z_lo) * 2 + y_hi) * 2 + core


def from_group(steps):
    pairs = []
    for y_lo in range(2):
        for x in range(4):
            for z_hi in range(8):
                for z_lo in range(2):
                    for y_hi in range(2):
                        for core in range(2):
                            s_lo, s_x = divmod((y_lo * 4 + x + steps[core]) % 8, 4)
                            y = y_hi * 2 + y_lo
                            if s_lo != y_lo:
                                y = (y + (1 if core == 0 else -1)) % 4
                            pairs.append((flat(s_lo, s_x, z_hi, z_lo, y // 2, core), flat(y_lo, x, z_hi, z_lo, y_hi, core)))
    return pairs


def call(body, outs, inputs, scratch=(), flops=0):
    size = sum(v.size * v.dtype.itemsize for v in inputs)
    whole = pl.BlockSpec(memory_space=pltpu.VMEM)
    return pl.pallas_call(
        body,
        out_shape=outs,
        in_specs=[pl.BlockSpec(memory_space=pltpu.SMEM) if v.dtype == jnp.int32 else whole for v in inputs],
        out_specs=jax.tree.map(lambda _: whole, outs),
        scratch_shapes=list(scratch),
        compiler_params=pltpu.CompilerParams(vmem_limit_bytes=VMEM),
        cost_estimate=pl.CostEstimate(flops=flops, bytes_accessed=size, transcendentals=0),
    )(*inputs)


def nt(left, right):
    return lax.dot_general(left, right, (((1,), (1,)), ((), ())), preferred_element_type=jnp.float32)


def inverse(values):
    floats = values.astype(jnp.float32)
    return lax.rsqrt(jnp.sum(floats * floats, axis=1, keepdims=True) + 1e-06)


def powered(inner, left_inv, right_inv):
    cosine = inner * left_inv * right_inv
    square = cosine * cosine
    return (KERNEL_VARIANCE * (square * square)).astype(jnp.bfloat16)


def halves_kernel(core, points, out, rest, sems):
    copies = []
    for i, (half, to) in enumerate(((core[0], out), (1 - core[0], rest))):
        rows = pl.ds(pl.multiple_of(half * HALF, HALF), HALF)
        copies.append(pltpu.make_async_copy(points.at[rows, :], to, sems.at[i]))
    for copy in copies:
        copy.start()
    for copy in copies:
        copy.wait()


def own_kernel(mine, rest, rows, out, rows_inv):
    mine_inv, rest_inv = inverse(mine[...]), inverse(rest[...])
    for i in range(ENV // 256):
        part = slice(i * 256, (i + 1) * 256)
        line = jnp.broadcast_to(inverse(rows[part, :]), (256, 128)).T[0:1, :]
        rows_inv[:, part] = line
        out[0:HALF, part] = powered(nt(mine[...], rows[part, :]), mine_inv, line)
        out[HALF:BLK, part] = powered(nt(rest[...], rows[part, :]), rest_inv, line)


def tile(left, right):
    return nt(left[0], right[0]) + nt(left[1], right[1])


def fill(points, inv, rows, rows_inv, out):
    for i in range(ENV // 256):
        part = slice(i * 256, (i + 1) * 256)
        out[:, part] = powered(nt(points[...], rows[part, :]), inv, rows_inv[:, part])


def second_kernel(mine, rest, rows, a1, a0, rows_inv, gram):
    own_kernel(mine, rest, rows, a0, rows_inv)
    gram[...] = tile((a0[...], a1[...]), (a0[0:HALF, :], a1[0:HALF, :]))


def next_kernel(b, d0, d1, e0, e1, a0, a1, gram, b0, b1):
    inv = inverse(b[...])
    fill(b, inv, d0, e0, b0)
    fill(b, inv, d1, e1, b1)
    gram[...] = tile((a0[...], a1[...]), (b0[...], b1[...]))


def exponent(largest):
    return jnp.floor(jnp.log2(jnp.maximum(largest, 1e-37)))


def coded(values, half):
    scaled = values * half * half
    scaled = scaled * scaled
    scaled = scaled * scaled
    return scaled * scaled


def marked(scaled, e, rows):
    row = lax.broadcasted_iota(jnp.int32, scaled.shape, 0)
    lane = lax.broadcasted_iota(jnp.int32, scaled.shape, 1)
    number = jnp.broadcast_to(e.astype(jnp.int32) + 128, scaled.shape)
    bit = lax.shift_right_logical(number, jnp.minimum(lane, 30)) & 1
    head = (row % rows == 0) & (lane < 8)
    scaled = jnp.where(head, jnp.maximum(scaled, 1e-35), scaled)
    return jnp.where(head & (bit == 1), -scaled, scaled)


def shift(head):
    floats = head.astype(jnp.float32)
    lane = lax.broadcasted_iota(jnp.int32, floats.shape, 1)
    weight = jnp.left_shift(1, jnp.minimum(lane, 7)).astype(jnp.float32)
    number = jnp.sum(jnp.where((lane < 8) & (floats < 0), weight, 0.0), axis=1, keepdims=True)
    return number - (128 + TARGET)


def decoded(values, add):
    return jnp.exp2(jnp.log2(jnp.abs(values.astype(jnp.float32))) * 0.125 + add)


def gram_kernel(core, g0, near, rest, a0, a1, b, d0, d1, e0, e1, out, b0, b1, g2):
    next_kernel(b, d0, d1, e0, e1, a0, a1, g2, b0, b1)
    sources = (g0, near, rest, g2)
    largest = jnp.zeros((1, HALF), jnp.float32)
    for source in sources:
        largest = jnp.maximum(largest, jnp.max(source[...], axis=0, keepdims=True))
    e = exponent(jnp.max(largest, axis=1, keepdims=True))
    half = jnp.exp2(0.5 * (TARGET - e))
    for d in range(8):
        for pair in range(4):
            starts = [lax.rem((2 * pair + i) * 64 + core[0] * HALF, BLK) + d * 8 for i in range(2)]
            starts = [pl.multiple_of(r, 8) for r in starts]
            to = slice(d * 64 + pair * 16, d * 64 + (pair + 1) * 16)
            for j, source in enumerate(sources):
                values = coded(jnp.concatenate([source[pl.ds(r, 8), :] for r in starts], axis=0), half)
                out[to, j * HALF : (j + 1) * HALF] = values.astype(jnp.bfloat16)
                if pair == 0 and j == 0:
                    out[to, 0:128] = marked(values[:, 0:128], e, 16).astype(jnp.bfloat16)


def middle_kernel(chunks, out):
    totals = []
    for core in range(2):
        total = jnp.zeros((64, WIDE), jnp.float32)
        for s in range(core, 8, 2):
            add = shift(chunks[s * 64 : s * 64 + 16, 0:128])[0:1]
            total = total + decoded(chunks[s * 64 : (s + 1) * 64, :], add)
        totals.append(total)
    largest = jnp.maximum(jnp.max(totals[0], axis=0, keepdims=True), jnp.max(totals[1], axis=0, keepdims=True))
    e = exponent(jnp.max(largest, axis=1, keepdims=True))
    half = jnp.exp2(0.5 * (TARGET - e))
    for core in range(2):
        values = coded(totals[core], half)
        out[:, core * WIDE : (core + 1) * WIDE] = values.astype(jnp.bfloat16)
        if core == 0:
            out[:, 0:128] = marked(values[:, 0:128], e, 8).astype(jnp.bfloat16)


def last_kernel(scale, chunks, out):
    adds = [shift(chunks[z_hi, :, 0:128])[0:1] for z_hi in range(8)]
    for core in range(2):
        near = 1 if core == 0 else 3
        for i, (j, half) in enumerate(((0, core), (near, core), (near, 1 - core), (2, core))):
            part = slice(core * WIDE + i * HALF, core * WIDE + (i + 1) * HALF)
            total = jnp.zeros((8, HALF), jnp.float32)
            for z_hi in range(8):
                total = total + decoded(chunks[z_hi, :, part], adds[z_hi])
            out[:, j * BLK + half * HALF : j * BLK + (half + 1) * HALF] = total * scale


def shards(descriptors, sparse_points):
    f32, bf16 = jnp.float32, jnp.bfloat16
    core = lax.axis_index("core")
    number = core.astype(jnp.int32).reshape(1)
    swap = [(0, 1), (1, 0)]
    one = jax.ShapeDtypeStruct((BLK, ENV), bf16)
    half = pltpu.VMEM((HALF, ENV), bf16)
    line = jax.ShapeDtypeStruct((1, ENV), f32)
    gram = jax.ShapeDtypeStruct((BLK, HALF), f32)
    work = 2 * BLK * ENV * D
    far = pl.BlockSpec(memory_space=pltpu.HBM)
    points_far = pltpu.with_memory_space_constraint(sparse_points, pltpu.HBM)
    whole = pl.BlockSpec(memory_space=pltpu.VMEM)
    mine, rest = pl.pallas_call(
        halves_kernel,
        out_shape=(jax.ShapeDtypeStruct((HALF, D), bf16), jax.ShapeDtypeStruct((HALF, D), bf16)),
        in_specs=[pl.BlockSpec(memory_space=pltpu.SMEM), far],
        out_specs=(whole, whole),
        scratch_shapes=[pltpu.SemaphoreType.DMA((2,))],
        compiler_params=pltpu.CompilerParams(vmem_limit_bytes=VMEM),
    )(number, points_far)
    near = [lax.ppermute(v, NAMES, from_group((1, 3))) for v in (mine, rest)]
    other = lax.ppermute(descriptors, "core", swap)
    a1, e1 = call(own_kernel, (one, line), (mine, rest, other), flops=work)
    a0, e0, g_aa = call(second_kernel, (one, line, gram), (mine, rest, descriptors, a1), flops=work * 3 // 2)
    near[0], e0 = lax.optimization_barrier((near[0], e0))
    far_points = lax.ppermute(near[0], NAMES, from_group((1, -1)))
    tiles = []
    for points in near:
        inputs = (points, descriptors, other, e0, e1, a0, a1)
        tiles.append(call(next_kernel, gram, inputs, [half, half], flops=work * 3 // 2))
    inputs = (number, g_aa, *tiles, a0, a1, far_points, descriptors, other, e0, e1)
    scratch = [half, half, pltpu.VMEM((BLK, HALF), f32)]
    sent = call(gram_kernel, jax.ShapeDtypeStruct((BLK, WIDE), bf16), inputs, scratch, flops=work * 3 // 2)
    got = lax.all_to_all(sent, ("z_lo", "y_hi", "core"), 0, 0, tiled=True)
    sent = call(middle_kernel, jax.ShapeDtypeStruct((64, 2 * WIDE), bf16), (got,))
    got = lax.all_to_all(sent.reshape(8, 8, 2 * WIDE), "z_hi", 0, 0, tiled=True)
    scale = 1.0 / (ENV * 64)
    out = jax.ShapeDtypeStruct((8, 4 * BLK), f32)
    return call(functools.partial(last_kernel, scale), out, (got,))


def solution(mesh):
    fine = Mesh(mesh.devices.reshape(SIZES), NAMES)
    return jax.shard_map(
        shards,
        mesh=fine,
        in_specs=(P(("z_hi", "z_lo", "y_hi", "core"), None), P(("y_lo", "x"), None)),
        out_specs=P(NAMES, None),
        check_vma=False,
    )
```

```python
import functools

import jax
import jax.numpy as jnp
from jax import lax
from jax.experimental import pallas as pl
from jax.experimental.pallas import tpu as pltpu
from jax.sharding import Mesh
from jax.sharding import PartitionSpec as P

NAMES = ("y_lo", "x", "z_hi", "z_lo", "y_hi", "core")
SIZES = (2, 4, 8, 2, 2, 2)
KERNEL_VARIANCE = 24.0
D = 1024
ENV = 1024
BLK = 512
HALF = BLK // 2
WIDE = 4 * HALF
TARGET = 14
VMEM = 24 * 1024 * 1024


def flat(y_lo, x, z_hi, z_lo, y_hi, core):
    return ((((y_lo * 4 + x) * 8 + z_hi) * 2 + z_lo) * 2 + y_hi) * 2 + core


def from_group(steps):
    pairs = []
    for y_lo in range(2):
        for x in range(4):
            for z_hi in range(8):
                for z_lo in range(2):
                    for y_hi in range(2):
                        for core in range(2):
                            s_lo, s_x = divmod((y_lo * 4 + x + steps[core]) % 8, 4)
                            y = y_hi * 2 + y_lo
                            if s_lo != y_lo:
                                y = (y + (1 if core == 0 else -1)) % 4
                            pairs.append((flat(s_lo, s_x, z_hi, z_lo, y // 2, core), flat(y_lo, x, z_hi, z_lo, y_hi, core)))
    return pairs


def call(body, outs, inputs, scratch=(), flops=0):
    size = sum(v.size * v.dtype.itemsize for v in inputs)
    whole = pl.BlockSpec(memory_space=pltpu.VMEM)
    return pl.pallas_call(
        body,
        out_shape=outs,
        in_specs=[pl.BlockSpec(memory_space=pltpu.SMEM) if v.dtype == jnp.int32 else whole for v in inputs],
        out_specs=jax.tree.map(lambda _: whole, outs),
        scratch_shapes=list(scratch),
        compiler_params=pltpu.CompilerParams(vmem_limit_bytes=VMEM),
        cost_estimate=pl.CostEstimate(flops=flops, bytes_accessed=size, transcendentals=0),
    )(*inputs)


def nt(left, right):
    return lax.dot_general(left, right, (((1,), (1,)), ((), ())), preferred_element_type=jnp.float32)


def inverse(values):
    floats = values.astype(jnp.float32)
    return lax.rsqrt(jnp.sum(floats * floats, axis=1, keepdims=True) + 1e-06)


def powered(inner, left_inv, right_inv):
    cosine = inner * left_inv * right_inv
    square = cosine * cosine
    return (KERNEL_VARIANCE * (square * square)).astype(jnp.bfloat16)


def halves_kernel(core, points, out, rest, sems):
    copies = []
    for i, (half, to) in enumerate(((core[0], out), (1 - core[0], rest))):
        rows = pl.ds(pl.multiple_of(half * HALF, HALF), HALF)
        copies.append(pltpu.make_async_copy(points.at[rows, :], to, sems.at[i]))
    for copy in copies:
        copy.start()
    for copy in copies:
        copy.wait()


def own_kernel(mine, rest, rows, out, rows_inv):
    mine_inv, rest_inv = inverse(mine[...]), inverse(rest[...])
    for i in range(ENV // 256):
        part = slice(i * 256, (i + 1) * 256)
        line = jnp.broadcast_to(inverse(rows[part, :]), (256, 128)).T[0:1, :]
        rows_inv[:, part] = line
        out[0:HALF, part] = powered(nt(mine[...], rows[part, :]), mine_inv, line)
        out[HALF:BLK, part] = powered(nt(rest[...], rows[part, :]), rest_inv, line)


def tile(left, right):
    return nt(left[0], right[0]) + nt(left[1], right[1])


def fill(points, inv, rows, rows_inv, out):
    for i in range(ENV // 256):
        part = slice(i * 256, (i + 1) * 256)
        out[:, part] = powered(nt(points[...], rows[part, :]), inv, rows_inv[:, part])


def second_kernel(mine, rest, rows, a1, a0, rows_inv, gram):
    own_kernel(mine, rest, rows, a0, rows_inv)
    gram[...] = tile((a0[...], a1[...]), (a0[0:HALF, :], a1[0:HALF, :]))


def next_kernel(b, d0, d1, e0, e1, a0, a1, gram, b0, b1):
    inv = inverse(b[...])
    fill(b, inv, d0, e0, b0)
    fill(b, inv, d1, e1, b1)
    gram[...] = tile((a0[...], a1[...]), (b0[...], b1[...]))


def exponent(largest):
    return jnp.floor(jnp.log2(jnp.maximum(largest, 1e-37)))


def coded(values, half):
    scaled = values * half * half
    scaled = scaled * scaled
    scaled = scaled * scaled
    return scaled * scaled


def marked(scaled, e, rows):
    row = lax.broadcasted_iota(jnp.int32, scaled.shape, 0)
    lane = lax.broadcasted_iota(jnp.int32, scaled.shape, 1)
    number = jnp.broadcast_to(e.astype(jnp.int32) + 128, scaled.shape)
    bit = lax.shift_right_logical(number, jnp.minimum(lane, 30)) & 1
    head = (row % rows == 0) & (lane < 8)
    scaled = jnp.where(head, jnp.maximum(scaled, 1e-35), scaled)
    return jnp.where(head & (bit == 1), -scaled, scaled)


def shift(head):
    floats = head.astype(jnp.float32)
    lane = lax.broadcasted_iota(jnp.int32, floats.shape, 1)
    weight = jnp.left_shift(1, jnp.minimum(lane, 7)).astype(jnp.float32)
    number = jnp.sum(jnp.where((lane < 8) & (floats < 0), weight, 0.0), axis=1, keepdims=True)
    return number - (128 + TARGET)


def decoded(values, add):
    return jnp.exp2(jnp.log2(jnp.abs(values.astype(jnp.float32))) * 0.125 + add)


def gram_kernel(core, g0, near, rest, a0, a1, b, d0, d1, e0, e1, out, b0, b1, g2):
    next_kernel(b, d0, d1, e0, e1, a0, a1, g2, b0, b1)
    sources = (g0, near, rest, g2)
    largest = jnp.zeros((1, HALF), jnp.float32)
    for source in sources:
        largest = jnp.maximum(largest, jnp.max(source[...], axis=0, keepdims=True))
    e = exponent(jnp.max(largest, axis=1, keepdims=True))
    half = jnp.exp2(0.5 * (TARGET - e))
    for d in range(8):
        for pair in range(4):
            starts = [lax.rem((2 * pair + i) * 64 + core[0] * HALF, BLK) + d * 8 for i in range(2)]
            starts = [pl.multiple_of(r, 8) for r in starts]
            to = slice(d * 64 + pair * 16, d * 64 + (pair + 1) * 16)
            for j, source in enumerate(sources):
                values = coded(jnp.concatenate([source[pl.ds(r, 8), :] for r in starts], axis=0), half)
                out[to, j * HALF : (j + 1) * HALF] = values.astype(jnp.bfloat16)
                if pair == 0 and j == 0:
                    out[to, 0:128] = marked(values[:, 0:128], e, 16).astype(jnp.bfloat16)


def middle_kernel(chunks, out):
    totals = []
    for core in range(2):
        total = jnp.zeros((64, WIDE), jnp.float32)
        for s in range(core, 8, 2):
            add = shift(chunks[s * 64 : s * 64 + 16, 0:128])[0:1]
            total = total + decoded(chunks[s * 64 : (s + 1) * 64, :], add)
        totals.append(total)
    largest = jnp.maximum(jnp.max(totals[0], axis=0, keepdims=True), jnp.max(totals[1], axis=0, keepdims=True))
    e = exponent(jnp.max(largest, axis=1, keepdims=True))
    half = jnp.exp2(0.5 * (TARGET - e))
    for core in range(2):
        values = coded(totals[core], half)
        out[:, core * WIDE : (core + 1) * WIDE] = values.astype(jnp.bfloat16)
        if core == 0:
            out[:, 0:128] = marked(values[:, 0:128], e, 8).astype(jnp.bfloat16)


def last_kernel(scale, chunks, out):
    adds = [shift(chunks[z_hi, :, 0:128])[0:1] for z_hi in range(8)]
    for core in range(2):
        near = 1 if core == 0 else 3
        for i, (j, half) in enumerate(((0, core), (near, core), (near, 1 - core), (2, core))):
            part = slice(core * WIDE + i * HALF, core * WIDE + (i + 1) * HALF)
            total = jnp.zeros((8, HALF), jnp.float32)
            for z_hi in range(8):
                total = total + decoded(chunks[z_hi, :, part], adds[z_hi])
            out[:, j * BLK + half * HALF : j * BLK + (half + 1) * HALF] = total * scale


def shards(descriptors, sparse_points):
    f32, bf16 = jnp.float32, jnp.bfloat16
    core = lax.axis_index("core")
    number = core.astype(jnp.int32).reshape(1)
    swap = [(0, 1), (1, 0)]
    one = jax.ShapeDtypeStruct((BLK, ENV), bf16)
    half = pltpu.VMEM((HALF, ENV), bf16)
    line = jax.ShapeDtypeStruct((1, ENV), f32)
    gram = jax.ShapeDtypeStruct((BLK, HALF), f32)
    work = 2 * BLK * ENV * D
    far = pl.BlockSpec(memory_space=pltpu.HBM)
    points_far = pltpu.with_memory_space_constraint(sparse_points, pltpu.HBM)
    whole = pl.BlockSpec(memory_space=pltpu.VMEM)
    mine, rest = pl.pallas_call(
        halves_kernel,
        out_shape=(jax.ShapeDtypeStruct((HALF, D), bf16), jax.ShapeDtypeStruct((HALF, D), bf16)),
        in_specs=[pl.BlockSpec(memory_space=pltpu.SMEM), far],
        out_specs=(whole, whole),
        scratch_shapes=[pltpu.SemaphoreType.DMA((2,))],
        compiler_params=pltpu.CompilerParams(vmem_limit_bytes=VMEM),
    )(number, points_far)
    near = [lax.ppermute(v, NAMES, from_group((1, 3))) for v in (mine, rest)]
    mine, rest, rows = lax.optimization_barrier((mine, rest, descriptors))
    other = lax.ppermute(rows, "core", swap)
    a1, e1 = call(own_kernel, (one, line), (mine, rest, other), flops=work)
    a0, e0, g_aa = call(second_kernel, (one, line, gram), (mine, rest, descriptors, a1), flops=work * 3 // 2)
    near[0], e0 = lax.optimization_barrier((near[0], e0))
    far_points = lax.ppermute(near[0], NAMES, from_group((1, -1)))
    tiles = []
    for points in near:
        inputs = (points, descriptors, other, e0, e1, a0, a1)
        tiles.append(call(next_kernel, gram, inputs, [half, half], flops=work * 3 // 2))
    inputs = (number, g_aa, *tiles, a0, a1, far_points, descriptors, other, e0, e1)
    scratch = [half, half, pltpu.VMEM((BLK, HALF), f32)]
    sent = call(gram_kernel, jax.ShapeDtypeStruct((BLK, WIDE), bf16), inputs, scratch, flops=work * 3 // 2)
    got = lax.all_to_all(sent, ("z_lo", "y_hi", "core"), 0, 0, tiled=True)
    sent = call(middle_kernel, jax.ShapeDtypeStruct((64, 2 * WIDE), bf16), (got,))
    got = lax.all_to_all(sent.reshape(8, 8, 2 * WIDE), "z_hi", 0, 0, tiled=True)
    scale = 1.0 / (ENV * 64)
    out = jax.ShapeDtypeStruct((8, 4 * BLK), f32)
    return call(functools.partial(last_kernel, scale), out, (got,))


def solution(mesh):
    fine = Mesh(mesh.devices.reshape(SIZES), NAMES)
    return jax.shard_map(
        shards,
        mesh=fine,
        in_specs=(P(("z_hi", "z_lo", "y_hi", "core"), None), P(("y_lo", "x"), None)),
        out_specs=P(NAMES, None),
        check_vma=False,
    )
```

```python
import functools

import jax
import jax.numpy as jnp
from jax import lax
from jax.experimental import pallas as pl
from jax.experimental.pallas import tpu as pltpu
from jax.sharding import Mesh
from jax.sharding import PartitionSpec as P

NAMES = ("y_lo", "x", "z_hi", "z_lo", "y_hi", "core")
SIZES = (2, 4, 8, 2, 2, 2)
KERNEL_VARIANCE = 24.0
D = 1024
ENV = 1024
BLK = 512
HALF = BLK // 2
WIDE = 4 * HALF
TARGET = 14
VMEM = 24 * 1024 * 1024


def flat(y_lo, x, z_hi, z_lo, y_hi, core):
    return ((((y_lo * 4 + x) * 8 + z_hi) * 2 + z_lo) * 2 + y_hi) * 2 + core


def from_group(steps):
    pairs = []
    for y_lo in range(2):
        for x in range(4):
            for z_hi in range(8):
                for z_lo in range(2):
                    for y_hi in range(2):
                        for core in range(2):
                            s_lo, s_x = divmod((y_lo * 4 + x + steps[core]) % 8, 4)
                            y = y_hi * 2 + y_lo
                            if s_lo != y_lo:
                                y = (y + (1 if core == 0 else -1)) % 4
                            pairs.append((flat(s_lo, s_x, z_hi, z_lo, y // 2, core), flat(y_lo, x, z_hi, z_lo, y_hi, core)))
    return pairs


def call(body, outs, inputs, scratch=(), flops=0):
    size = sum(v.size * v.dtype.itemsize for v in inputs)
    whole = pl.BlockSpec(memory_space=pltpu.VMEM)
    return pl.pallas_call(
        body,
        out_shape=outs,
        in_specs=[pl.BlockSpec(memory_space=pltpu.SMEM) if v.dtype == jnp.int32 else whole for v in inputs],
        out_specs=jax.tree.map(lambda _: whole, outs),
        scratch_shapes=list(scratch),
        compiler_params=pltpu.CompilerParams(vmem_limit_bytes=VMEM),
        cost_estimate=pl.CostEstimate(flops=flops, bytes_accessed=size, transcendentals=0),
    )(*inputs)


def nt(left, right):
    return lax.dot_general(left, right, (((1,), (1,)), ((), ())), preferred_element_type=jnp.float32)


def inverse(values):
    floats = values.astype(jnp.float32)
    return lax.rsqrt(jnp.sum(floats * floats, axis=1, keepdims=True) + 1e-06)


def powered(inner, left_inv, right_inv):
    cosine = inner * left_inv * right_inv
    square = cosine * cosine
    return (KERNEL_VARIANCE * (square * square)).astype(jnp.bfloat16)


def halves_kernel(core, points, out, rest, sems):
    copies = []
    for i, (half, to) in enumerate(((core[0], out), (1 - core[0], rest))):
        rows = pl.ds(pl.multiple_of(half * HALF, HALF), HALF)
        copies.append(pltpu.make_async_copy(points.at[rows, :], to, sems.at[i]))
    for copy in copies:
        copy.start()
    for copy in copies:
        copy.wait()


def own_kernel(mine, rest, rows, out, rows_inv):
    mine_inv, rest_inv = inverse(mine[...]), inverse(rest[...])
    for i in range(ENV // 256):
        part = slice(i * 256, (i + 1) * 256)
        line = jnp.broadcast_to(inverse(rows[part, :]), (256, 128)).T[0:1, :]
        rows_inv[:, part] = line
        out[0:HALF, part] = powered(nt(mine[...], rows[part, :]), mine_inv, line)
        out[HALF:BLK, part] = powered(nt(rest[...], rows[part, :]), rest_inv, line)


def tile(left, right):
    return nt(left[0], right[0]) + nt(left[1], right[1])


def fill(points, inv, rows, rows_inv, out):
    for i in range(ENV // 512):
        part = slice(i * 512, (i + 1) * 512)
        out[:, part] = powered(nt(points[...], rows[part, :]), inv, rows_inv[:, part])


def second_kernel(mine, rest, rows, a1, a0, rows_inv, gram):
    own_kernel(mine, rest, rows, a0, rows_inv)
    gram[...] = tile((a0[...], a1[...]), (a0[0:HALF, :], a1[0:HALF, :]))


def next_kernel(b, d0, d1, e0, e1, a0, a1, gram, b0, b1):
    inv = inverse(b[...])
    fill(b, inv, d0, e0, b0)
    fill(b, inv, d1, e1, b1)
    gram[...] = tile((a0[...], a1[...]), (b0[...], b1[...]))


def exponent(largest):
    return jnp.floor(jnp.log2(jnp.maximum(largest, 1e-37)))


def coded(values, half):
    scaled = values * half * half
    scaled = scaled * scaled
    scaled = scaled * scaled
    return scaled * scaled


def marked(scaled, e, rows):
    row = lax.broadcasted_iota(jnp.int32, scaled.shape, 0)
    lane = lax.broadcasted_iota(jnp.int32, scaled.shape, 1)
    number = jnp.broadcast_to(e.astype(jnp.int32) + 128, scaled.shape)
    bit = lax.shift_right_logical(number, jnp.minimum(lane, 30)) & 1
    head = (row % rows == 0) & (lane < 8)
    scaled = jnp.where(head, jnp.maximum(scaled, 1e-35), scaled)
    return jnp.where(head & (bit == 1), -scaled, scaled)


def shift(head):
    floats = head.astype(jnp.float32)
    lane = lax.broadcasted_iota(jnp.int32, floats.shape, 1)
    weight = jnp.left_shift(1, jnp.minimum(lane, 7)).astype(jnp.float32)
    number = jnp.sum(jnp.where((lane < 8) & (floats < 0), weight, 0.0), axis=1, keepdims=True)
    return number - (128 + TARGET)


def decoded(values, add):
    return jnp.exp2(jnp.log2(jnp.abs(values.astype(jnp.float32))) * 0.125 + add)


def gram_kernel(core, g0, near, rest, a0, a1, b, d0, d1, e0, e1, out, b0, b1, g2):
    next_kernel(b, d0, d1, e0, e1, a0, a1, g2, b0, b1)
    sources = (g0, near, rest, g2)
    largest = jnp.zeros((1, HALF), jnp.float32)
    for source in sources:
        largest = jnp.maximum(largest, jnp.max(source[...], axis=0, keepdims=True))
    e = exponent(jnp.max(largest, axis=1, keepdims=True))
    half = jnp.exp2(0.5 * (TARGET - e))
    for d in range(8):
        for pair in range(4):
            starts = [lax.rem((2 * pair + i) * 64 + core[0] * HALF, BLK) + d * 8 for i in range(2)]
            starts = [pl.multiple_of(r, 8) for r in starts]
            to = slice(d * 64 + pair * 16, d * 64 + (pair + 1) * 16)
            for j, source in enumerate(sources):
                values = coded(jnp.concatenate([source[pl.ds(r, 8), :] for r in starts], axis=0), half)
                out[to, j * HALF : (j + 1) * HALF] = values.astype(jnp.bfloat16)
                if pair == 0 and j == 0:
                    out[to, 0:128] = marked(values[:, 0:128], e, 16).astype(jnp.bfloat16)


def middle_kernel(chunks, out):
    totals = []
    for core in range(2):
        total = jnp.zeros((64, WIDE), jnp.float32)
        for s in range(core, 8, 2):
            add = shift(chunks[s * 64 : s * 64 + 16, 0:128])[0:1]
            total = total + decoded(chunks[s * 64 : (s + 1) * 64, :], add)
        totals.append(total)
    largest = jnp.maximum(jnp.max(totals[0], axis=0, keepdims=True), jnp.max(totals[1], axis=0, keepdims=True))
    e = exponent(jnp.max(largest, axis=1, keepdims=True))
    half = jnp.exp2(0.5 * (TARGET - e))
    for core in range(2):
        values = coded(totals[core], half)
        out[:, core * WIDE : (core + 1) * WIDE] = values.astype(jnp.bfloat16)
        if core == 0:
            out[:, 0:128] = marked(values[:, 0:128], e, 8).astype(jnp.bfloat16)


def last_kernel(scale, chunks, out):
    adds = [shift(chunks[z_hi, :, 0:128])[0:1] for z_hi in range(8)]
    for core in range(2):
        near = 1 if core == 0 else 3
        for i, (j, half) in enumerate(((0, core), (near, core), (near, 1 - core), (2, core))):
            part = slice(core * WIDE + i * HALF, core * WIDE + (i + 1) * HALF)
            total = jnp.zeros((8, HALF), jnp.float32)
            for z_hi in range(8):
                total = total + decoded(chunks[z_hi, :, part], adds[z_hi])
            out[:, j * BLK + half * HALF : j * BLK + (half + 1) * HALF] = total * scale


def shards(descriptors, sparse_points):
    f32, bf16 = jnp.float32, jnp.bfloat16
    core = lax.axis_index("core")
    number = core.astype(jnp.int32).reshape(1)
    swap = [(0, 1), (1, 0)]
    one = jax.ShapeDtypeStruct((BLK, ENV), bf16)
    half = pltpu.VMEM((HALF, ENV), bf16)
    line = jax.ShapeDtypeStruct((1, ENV), f32)
    gram = jax.ShapeDtypeStruct((BLK, HALF), f32)
    work = 2 * BLK * ENV * D
    far = pl.BlockSpec(memory_space=pltpu.HBM)
    points_far = pltpu.with_memory_space_constraint(sparse_points, pltpu.HBM)
    whole = pl.BlockSpec(memory_space=pltpu.VMEM)
    mine, rest = pl.pallas_call(
        halves_kernel,
        out_shape=(jax.ShapeDtypeStruct((HALF, D), bf16), jax.ShapeDtypeStruct((HALF, D), bf16)),
        in_specs=[pl.BlockSpec(memory_space=pltpu.SMEM), far],
        out_specs=(whole, whole),
        scratch_shapes=[pltpu.SemaphoreType.DMA((2,))],
        compiler_params=pltpu.CompilerParams(vmem_limit_bytes=VMEM),
    )(number, points_far)
    near = [lax.ppermute(v, NAMES, from_group((1, 3))) for v in (mine, rest)]
    mine, rest, rows = lax.optimization_barrier((mine, rest, descriptors))
    other = lax.ppermute(rows, "core", swap)
    a1, e1 = call(own_kernel, (one, line), (mine, rest, other), flops=work)
    near[0], e1 = lax.optimization_barrier((near[0], e1))
    far_points = lax.ppermute(near[0], NAMES, from_group((1, -1)))
    a0, e0, g_aa = call(second_kernel, (one, line, gram), (mine, rest, descriptors, a1), flops=work * 3 // 2)
    tiles = []
    for points in near:
        inputs = (points, descriptors, other, e0, e1, a0, a1)
        tiles.append(call(next_kernel, gram, inputs, [half, half], flops=work * 3 // 2))
    inputs = (number, g_aa, *tiles, a0, a1, far_points, descriptors, other, e0, e1)
    scratch = [half, half, pltpu.VMEM((BLK, HALF), f32)]
    sent = call(gram_kernel, jax.ShapeDtypeStruct((BLK, WIDE), bf16), inputs, scratch, flops=work * 3 // 2)
    got = lax.all_to_all(sent, ("z_lo", "y_hi", "core"), 0, 0, tiled=True)
    sent = call(middle_kernel, jax.ShapeDtypeStruct((64, 2 * WIDE), bf16), (got,))
    got = lax.all_to_all(sent.reshape(8, 8, 2 * WIDE), "z_hi", 0, 0, tiled=True)
    scale = 1.0 / (ENV * 64)
    out = jax.ShapeDtypeStruct((8, 4 * BLK), f32)
    return call(functools.partial(last_kernel, scale), out, (got,))


def solution(mesh):
    fine = Mesh(mesh.devices.reshape(SIZES), NAMES)
    return jax.shard_map(
        shards,
        mesh=fine,
        in_specs=(P(("z_hi", "z_lo", "y_hi", "core"), None), P(("y_lo", "x"), None)),
        out_specs=P(NAMES, None),
        check_vma=False,
    )
```

```python
import functools

import jax
import jax.numpy as jnp
from jax import lax
from jax.experimental import pallas as pl
from jax.experimental.pallas import tpu as pltpu
from jax.sharding import Mesh
from jax.sharding import PartitionSpec as P

NAMES = ("y_lo", "x", "z_hi", "z_lo", "y_hi", "core")
SIZES = (2, 4, 8, 2, 2, 2)
KERNEL_VARIANCE = 24.0
D = 1024
ENV = 1024
BLK = 512
HALF = BLK // 2
WIDE = 4 * HALF
TARGET = 14
VMEM = 24 * 1024 * 1024


def flat(y_lo, x, z_hi, z_lo, y_hi, core):
    return ((((y_lo * 4 + x) * 8 + z_hi) * 2 + z_lo) * 2 + y_hi) * 2 + core


def from_group(steps):
    pairs = []
    for y_lo in range(2):
        for x in range(4):
            for z_hi in range(8):
                for z_lo in range(2):
                    for y_hi in range(2):
                        for core in range(2):
                            s_lo, s_x = divmod((y_lo * 4 + x + steps[core]) % 8, 4)
                            y = y_hi * 2 + y_lo
                            if s_lo != y_lo:
                                y = (y + (1 if core == 0 else -1)) % 4
                            pairs.append((flat(s_lo, s_x, z_hi, z_lo, y // 2, core), flat(y_lo, x, z_hi, z_lo, y_hi, core)))
    return pairs


def call(body, outs, inputs, scratch=(), flops=0):
    size = sum(v.size * v.dtype.itemsize for v in inputs)
    whole = pl.BlockSpec(memory_space=pltpu.VMEM)
    return pl.pallas_call(
        body,
        out_shape=outs,
        in_specs=[pl.BlockSpec(memory_space=pltpu.SMEM) if v.dtype == jnp.int32 else whole for v in inputs],
        out_specs=jax.tree.map(lambda _: whole, outs),
        scratch_shapes=list(scratch),
        compiler_params=pltpu.CompilerParams(vmem_limit_bytes=VMEM),
        cost_estimate=pl.CostEstimate(flops=flops, bytes_accessed=size, transcendentals=0),
    )(*inputs)


def nt(left, right):
    return lax.dot_general(left, right, (((1,), (1,)), ((), ())), preferred_element_type=jnp.float32)


def inverse(values):
    floats = values.astype(jnp.float32)
    return lax.rsqrt(jnp.sum(floats * floats, axis=1, keepdims=True) + 1e-06)


def powered(inner, left_inv, right_inv):
    cosine = inner * left_inv * right_inv
    square = cosine * cosine
    return (KERNEL_VARIANCE * (square * square)).astype(jnp.bfloat16)


def half_kernel(half, points, out, sem):
    rows = pl.ds(pl.multiple_of(half[0] * HALF, HALF), HALF)
    copy = pltpu.make_async_copy(points.at[rows, :], out, sem)
    copy.start()
    copy.wait()


def own_kernel(mine, rest, rows, out, rows_inv):
    mine_inv, rest_inv = inverse(mine[...]), inverse(rest[...])
    for i in range(ENV // 256):
        part = slice(i * 256, (i + 1) * 256)
        line = jnp.broadcast_to(inverse(rows[part, :]), (256, 128)).T[0:1, :]
        rows_inv[:, part] = line
        out[0:HALF, part] = powered(nt(mine[...], rows[part, :]), mine_inv, line)
        out[HALF:BLK, part] = powered(nt(rest[...], rows[part, :]), rest_inv, line)


def tile(left, right):
    return nt(left[0], right[0]) + nt(left[1], right[1])


def fill(points, inv, rows, rows_inv, out):
    for i in range(ENV // 512):
        part = slice(i * 512, (i + 1) * 512)
        out[:, part] = powered(nt(points[...], rows[part, :]), inv, rows_inv[:, part])


def second_kernel(mine, rest, rows, a1, a0, rows_inv, gram):
    own_kernel(mine, rest, rows, a0, rows_inv)
    gram[...] = tile((a0[...], a1[...]), (a0[0:HALF, :], a1[0:HALF, :]))


def next_kernel(b, d0, d1, e0, e1, a0, a1, gram, b0, b1):
    inv = inverse(b[...])
    fill(b, inv, d0, e0, b0)
    fill(b, inv, d1, e1, b1)
    gram[...] = tile((a0[...], a1[...]), (b0[...], b1[...]))


def exponent(largest):
    return jnp.floor(jnp.log2(jnp.maximum(largest, 1e-37)))


def coded(values, half):
    scaled = values * half * half
    scaled = scaled * scaled
    scaled = scaled * scaled
    return scaled * scaled


def marked(scaled, e, rows):
    row = lax.broadcasted_iota(jnp.int32, scaled.shape, 0)
    lane = lax.broadcasted_iota(jnp.int32, scaled.shape, 1)
    number = jnp.broadcast_to(e.astype(jnp.int32) + 128, scaled.shape)
    bit = lax.shift_right_logical(number, jnp.minimum(lane, 30)) & 1
    head = (row % rows == 0) & (lane < 8)
    scaled = jnp.where(head, jnp.maximum(scaled, 1e-35), scaled)
    return jnp.where(head & (bit == 1), -scaled, scaled)


def shift(head):
    floats = head.astype(jnp.float32)
    lane = lax.broadcasted_iota(jnp.int32, floats.shape, 1)
    weight = jnp.left_shift(1, jnp.minimum(lane, 7)).astype(jnp.float32)
    number = jnp.sum(jnp.where((lane < 8) & (floats < 0), weight, 0.0), axis=1, keepdims=True)
    return number - (128 + TARGET)


def decoded(values, add):
    return jnp.exp2(jnp.log2(jnp.abs(values.astype(jnp.float32))) * 0.125 + add)


def gram_kernel(core, g0, near, rest, a0, a1, b, d0, d1, e0, e1, out, b0, b1, g2):
    next_kernel(b, d0, d1, e0, e1, a0, a1, g2, b0, b1)
    sources = (g0, near, rest, g2)
    largest = jnp.zeros((1, HALF), jnp.float32)
    for source in sources:
        largest = jnp.maximum(largest, jnp.max(source[...], axis=0, keepdims=True))
    e = exponent(jnp.max(largest, axis=1, keepdims=True))
    half = jnp.exp2(0.5 * (TARGET - e))
    for d in range(8):
        for pair in range(4):
            starts = [lax.rem((2 * pair + i) * 64 + core[0] * HALF, BLK) + d * 8 for i in range(2)]
            starts = [pl.multiple_of(r, 8) for r in starts]
            to = slice(d * 64 + pair * 16, d * 64 + (pair + 1) * 16)
            for j, source in enumerate(sources):
                values = coded(jnp.concatenate([source[pl.ds(r, 8), :] for r in starts], axis=0), half)
                out[to, j * HALF : (j + 1) * HALF] = values.astype(jnp.bfloat16)
                if pair == 0 and j == 0:
                    out[to, 0:128] = marked(values[:, 0:128], e, 16).astype(jnp.bfloat16)


def middle_kernel(chunks, out):
    totals = []
    for core in range(2):
        total = jnp.zeros((64, WIDE), jnp.float32)
        for s in range(core, 8, 2):
            add = shift(chunks[s * 64 : s * 64 + 16, 0:128])[0:1]
            total = total + decoded(chunks[s * 64 : (s + 1) * 64, :], add)
        totals.append(total)
    largest = jnp.maximum(jnp.max(totals[0], axis=0, keepdims=True), jnp.max(totals[1], axis=0, keepdims=True))
    e = exponent(jnp.max(largest, axis=1, keepdims=True))
    half = jnp.exp2(0.5 * (TARGET - e))
    for core in range(2):
        values = coded(totals[core], half)
        out[:, core * WIDE : (core + 1) * WIDE] = values.astype(jnp.bfloat16)
        if core == 0:
            out[:, 0:128] = marked(values[:, 0:128], e, 8).astype(jnp.bfloat16)


def last_kernel(scale, chunks, out):
    adds = [shift(chunks[z_hi, :, 0:128])[0:1] for z_hi in range(8)]
    for core in range(2):
        near = 1 if core == 0 else 3
        for i, (j, half) in enumerate(((0, core), (near, core), (near, 1 - core), (2, core))):
            part = slice(core * WIDE + i * HALF, core * WIDE + (i + 1) * HALF)
            total = jnp.zeros((8, HALF), jnp.float32)
            for z_hi in range(8):
                total = total + decoded(chunks[z_hi, :, part], adds[z_hi])
            out[:, j * BLK + half * HALF : j * BLK + (half + 1) * HALF] = total * scale


def shards(descriptors, sparse_points):
    f32, bf16 = jnp.float32, jnp.bfloat16
    core = lax.axis_index("core")
    number = core.astype(jnp.int32).reshape(1)
    swap = [(0, 1), (1, 0)]
    one = jax.ShapeDtypeStruct((BLK, ENV), bf16)
    half = pltpu.VMEM((HALF, ENV), bf16)
    line = jax.ShapeDtypeStruct((1, ENV), f32)
    gram = jax.ShapeDtypeStruct((BLK, HALF), f32)
    work = 2 * BLK * ENV * D
    far = pl.BlockSpec(memory_space=pltpu.HBM)
    points_far = pltpu.with_memory_space_constraint(sparse_points, pltpu.HBM)
    whole = pl.BlockSpec(memory_space=pltpu.VMEM)
    mine, rest = (
        pl.pallas_call(
            half_kernel,
            out_shape=jax.ShapeDtypeStruct((HALF, D), bf16),
            in_specs=[pl.BlockSpec(memory_space=pltpu.SMEM), far],
            out_specs=whole,
            scratch_shapes=[pltpu.SemaphoreType.DMA],
            compiler_params=pltpu.CompilerParams(vmem_limit_bytes=VMEM),
        )(i, points_far)
        for i in (number, 1 - number)
    )
    near = [lax.ppermute(v, NAMES, from_group((1, 3))) for v in (mine, rest)]
    mine, rows = lax.optimization_barrier((mine, descriptors))
    other = lax.ppermute(rows, "core", swap)
    a1, e1 = call(own_kernel, (one, line), (mine, rest, other), flops=work)
    near[0], e1 = lax.optimization_barrier((near[0], e1))
    far_points = lax.ppermute(near[0], NAMES, from_group((1, -1)))
    a0, e0, g_aa = call(second_kernel, (one, line, gram), (mine, rest, descriptors, a1), flops=work * 3 // 2)
    tiles = []
    for points in near:
        inputs = (points, descriptors, other, e0, e1, a0, a1)
        tiles.append(call(next_kernel, gram, inputs, [half, half], flops=work * 3 // 2))
    inputs = (number, g_aa, *tiles, a0, a1, far_points, descriptors, other, e0, e1)
    scratch = [half, half, pltpu.VMEM((BLK, HALF), f32)]
    sent = call(gram_kernel, jax.ShapeDtypeStruct((BLK, WIDE), bf16), inputs, scratch, flops=work * 3 // 2)
    got = lax.all_to_all(sent, ("z_lo", "y_hi", "core"), 0, 0, tiled=True)
    sent = call(middle_kernel, jax.ShapeDtypeStruct((64, 2 * WIDE), bf16), (got,))
    got = lax.all_to_all(sent.reshape(8, 8, 2 * WIDE), "z_hi", 0, 0, tiled=True)
    scale = 1.0 / (ENV * 64)
    out = jax.ShapeDtypeStruct((8, 4 * BLK), f32)
    return call(functools.partial(last_kernel, scale), out, (got,))


def solution(mesh):
    fine = Mesh(mesh.devices.reshape(SIZES), NAMES)
    return jax.shard_map(
        shards,
        mesh=fine,
        in_specs=(P(("z_hi", "z_lo", "y_hi", "core"), None), P(("y_lo", "x"), None)),
        out_specs=P(NAMES, None),
        check_vma=False,
    )
```
